512 devices in a mesh: row: 16 (over y_hi, x, core), col: 32 (over y_lo, z).
Axes of the slice: x: 4, y: 8 (y_hi: 2, y_lo: 4; y = y_hi * 4 + y_lo), z: 8, core: 2. Of those that a mesh axis runs over, the one named last changes fastest.
Arguments:
- ci_coeffs: float32 [8192, 8192], P('row', 'col'), may hold values from -6 to 6
- h_blocks: float32 [64, 24, 128, 128], P('col'), may hold values from -0.109375 to 0.109375
- block_columns: int32 [64, 24], P('col'), may hold values from 0 to 63, as said below
Outputs:
- sigma: float32 [8192, 8192], P('row', 'col')
The draws below stay inside these ranges and needn't reach their ends.
Inputs may be any that keep to these rules, and one draw needn't show every extreme that they name: `block_columns`: block row J lists 24 different block columns, J itself among them, each of the form (J + t) modulo 64 with -16 <= t < 16.
All inputs are finite; a program needn't handle non-finite values.
Results may differ from the reference program's by a relative error of at most 0.0001.
Values sent between devices are 32-bit elements; how exact they have to be, the bound alone decides.
A program may use at most 64 MiB of HBM per device.

```python
import jax
import jax.numpy as jnp
from jax import lax

BS = 128
K = 24
HALF = 16
NBLK = 64
N = 8192


def draw_block_columns(key, part):
    breadth = 2 * HALF - 1
    scores = jax.random.randint(key, (NBLK, breadth), 0, 2 ** 20) * breadth + jnp.arange(breadth, dtype=jnp.int32)[None, :]
    ranking = jnp.argsort(scores, axis=1)
    chosen = ranking[:, :K - 1]
    shifted = chosen - HALF + (chosen >= HALF).astype(jnp.int32)
    offsets = jnp.concatenate([jnp.zeros((NBLK, 1), jnp.int32), shifted], axis=1)
    columns = (jnp.arange(NBLK, dtype=jnp.int32)[:, None] + offsets) % NBLK
    return jnp.sort(columns, axis=1).astype(jnp.int32)


def steps_of(key, extent, shards, smallest, high):
    loudness, own = 1.0, jax.random.fold_in(key, 6)
    for dim, parts in shards:
        steps = jnp.exp(jax.random.uniform(jax.random.fold_in(own, dim), (parts,), jnp.float32, smallest / len(shards), high / len(shards)))
        loudness = loudness * jnp.repeat(steps, extent[dim] // parts).reshape([-1 if axis == dim else 1 for axis in range(len(extent))])
    return loudness


def bell_draw(key, shape, spread, bound, shards=(), held_as=jnp.bfloat16):
    entries = jax.random.normal(key, shape, jnp.float32) * spread
    if len(shards) > 0:
        entries = steps_of(key, shape, shards, -0.22, 0.18) * entries
    return jnp.clip(entries, min=-bound, max=bound).astype(held_as)


def setup_inputs(seed: int = 0) -> dict:
    key_of = jax.random.split(jax.random.key(seed), 4)
    return {
        "ci_coeffs": bell_draw(key_of[0], (N, N), 1.0, 6.0, ((0, 16), (1, 32)), jnp.float32),
        "h_blocks": bell_draw(key_of[1], (NBLK, K, BS, BS), (K * BS) ** -0.5, 0.109375, ((0, 32),), jnp.float32),
        "block_columns": draw_block_columns(jax.random.fold_in(key_of[3], 71), 0),
    }


def reference(ci_coeffs, h_blocks, block_columns):
    strings = NBLK * BS
    column_blocks = jnp.transpose(ci_coeffs.reshape(strings, NBLK, BS), (1, 0, 2))

    def accumulate(running, inputs):
        column_block, blocks_row, targets = inputs
        products = jnp.einsum("nb,kbe->kne", column_block, blocks_row, precision=lax.Precision.HIGHEST)
        return running.at[targets].add(products), None

    initial = jnp.zeros((NBLK, strings, BS), jnp.float32)
    gathered, unused = lax.scan(accumulate, initial, (column_blocks, h_blocks, block_columns))
    half_sigma = jnp.transpose(gathered, (1, 0, 2)).reshape(strings, strings)
    return half_sigma + half_sigma.T
```

```python
import jax
import jax.numpy as jnp
from jax import lax
from jax.experimental import pallas as pl
from jax.experimental.pallas import tpu as pltpu
from jax.sharding import PartitionSpec as P

NX, NYL, NZ = 4, 4, 8
BS = 128
K = 24
CH = 4
ROWS = 512
COLS = 256
QR = ROWS // CH
OFFS = 36
MESH = pl.DeviceIdType.MESH
ORDER = (4, 3, 5, 2, 6, 1, 7, 0, 8)
STAGGER = 1


def split(value):
    high = value.astype(jnp.bfloat16)
    low = (value - high.astype(jnp.float32)).astype(jnp.bfloat16)
    return high, low


def dot(a, b):
    return jnp.dot(a, b, preferred_element_type=jnp.float32)


def kernel(
    where_ref, flag_ref, c_hbm, h_hbm, out_ref,
    cbuf, hraw, placed, hy, wown, wnear, xb, first, plus, minus, final, mirrored,
    loc_sem, yc_send, yc_recv, yh_send, yh_recv, xh_send, xh_recv, kh_send, kh_recv,
    zp_send, zp_recv, zm_send, zm_recv, m_send, m_recv,
):
    r = lax.axis_index("row")
    c = lax.axis_index("col")
    y_hi, x, core = r // 8, (r // 2) % NX, r % 2
    y_lo, z = c // NZ, c % NZ
    y = y_hi * NYL + y_lo

    def physical(step):
        other = (y + step + 2 * NYL) % (2 * NYL)
        return (other // NYL) * 8 + x * 2 + core, (other % NYL) * NZ + z

    def along_x(step):
        return y_hi * 8 + ((x + step) % NX) * 2 + core, c

    col_above = (r, ((y_lo + 1) % NYL) * NZ + z)
    col_below = (r, ((y_lo + NYL - 1) % NYL) * NZ + z)
    y_above, y_below = physical(1), physical(-1)
    z_above = (r, y_lo * NZ + (z + 1) % NZ)
    z_below = (r, y_lo * NZ + (z + NZ - 1) % NZ)
    sibling = (y_hi * 8 + x * 2 + 1 - core, c)
    peers = [along_x(step) for step in (1, 2, 3)]
    on_diagonal = (c // 2 == r).astype(jnp.int32)

    get_c = pltpu.make_async_copy(c_hbm, cbuf.at[0], loc_sem.at[0])
    get_h = pltpu.make_async_copy(h_hbm, hraw, loc_sem.at[1])
    get_c.start()
    get_h.start()

    barrier = pltpu.get_barrier_semaphore()
    fixed = [col_above, col_below, y_above, y_below, z_above, z_below, sibling] + peers
    for device in fixed:
        pl.semaphore_signal(barrier, inc=1, device_id=device, device_id_type=MESH)
    for half in range(2):
        @pl.when(jnp.logical_not((c // 2 == r) & (c % 2 == half)))
        def _():
            pl.semaphore_signal(barrier, inc=1, device_id=(c // 2, 2 * r + half), device_id_type=MESH)
    get_c.wait()
    get_h.wait()
    pl.semaphore_wait(barrier, len(fixed) + 2 - on_diagonal)

    sends = []

    def remote(src, dst, send_sem, recv_sem, device):
        copy = pltpu.make_async_remote_copy(
            src_ref=src, dst_ref=dst, send_sem=send_sem, recv_sem=recv_sem,
            device_id=device, device_id_type=MESH,
        )
        copy.start()
        sends.append(copy)

    def arrived(ref, sem):
        pltpu.make_async_copy(ref, ref, sem).wait()

    def rows(q):
        return pl.ds(q * QR, QR)

    def send_c(q):
        remote(cbuf.at[0, rows(q)], cbuf.at[2, rows(q)], yc_send.at[0, q], yc_recv.at[1, q], col_above)
        remote(cbuf.at[0, rows(q)], cbuf.at[1, rows(q)], yc_send.at[1, q], yc_recv.at[0, q], col_below)

    def place(index):
        for j in range(2):
            for e in range(2):
                at = 2 * (index - 8) + e - j + 17
                block = hraw[j, where_ref[j, at]] * flag_ref[j, at]
                placed[index, 2 * j:2 * j + 2, :, :, e * BS:(e + 1) * BS] = block.reshape(2, 2, 32, BS)

    def inside(d):
        return z + d < NZ

    def send_h(slot):
        if slot == 0:
            index, device = 0, y_below
        elif slot == 8:
            index, device = 16, y_above
        else:
            index = jnp.where(inside(slot), slot, slot + 8)
            device = tuple(jnp.where(inside(slot), b, a) for a, b in zip(y_above, y_below))
        remote(placed.at[index, x, core], hy.at[slot, x, core], yh_send.at[slot], yh_recv.at[slot], device)

    send_c(0)
    for slot in ORDER:
        if slot == 8:
            place(16)
        else:
            place(slot)
            place(slot + 8)
        send_h(slot)
    for q in range(1, CH):
        send_c(q)

    def spread_x(slot):
        arrived(hy.at[slot, x, core], yh_recv.at[slot])
        for step in range(3):
            remote(hy.at[slot, x, core], hy.at[slot, x, core], xh_send.at[slot, step], xh_recv.at[slot, step], peers[step])

    def spread_core(slot):
        for step in range(3):
            arrived(hy.at[slot, 0, 0], xh_recv.at[slot, step])
        remote(hy.at[slot, :, core], hy.at[slot, :, core], kh_send.at[slot], kh_recv.at[slot], sibling)

    def split_own(d):
        index = 8 if d == 0 else jnp.where(inside(d), d + 8, d)
        high, low = split(placed[index].reshape(COLS, COLS))
        wown[d, 0] = high
        wown[d, 1] = low

    def split_near(slot):
        arrived(hy.at[slot, :, 0], kh_recv.at[slot])
        high, low = split(hy[slot].reshape(COLS, COLS))
        wnear[slot, 0] = high
        wnear[slot, 1] = low

    def split_c(which, q):
        high, low = split(cbuf[which, rows(q)])
        xb[which, 0, rows(q)] = high
        xb[which, 1, rows(q)] = low

    for slot in ORDER:
        if slot < 8:
            split_own(slot)
    for q in range(CH):
        split_c(0, q)

    ready = []

    def advance(upto):
        while len(ready) < upto:
            at = len(ready)
            for lead, stage in ((2, spread_x), (1, spread_core), (0, split_near)):
                low = 0 if at == 0 else at + lead
                for position in range(low, min(at + lead + 1, len(ORDER))):
                    stage(ORDER[position])
            ready.append(at)

    def product(which, weights, q):
        high, low = xb[which, 0, rows(q)], xb[which, 1, rows(q)]
        return dot(high, weights[0]) + dot(high, weights[1]) + dot(low, weights[0])

    def partial(q, d):
        total = product(0, wown.at[d], q)
        if d == 0:
            return total + product(1, wnear.at[0], q) + product(2, wnear.at[8], q)
        return total + product(jnp.where(inside(d), 1, 2), wnear.at[d], q)

    def lengths(q):
        return (4, 3) if q % 2 == 0 else (3, 4)

    def step_of(q, s):
        if s == 0:
            for which in (1, 2):
                arrived(cbuf.at[which, rows(q)], yc_recv.at[which - 1, q])
                split_c(which, q)
        need = {0: 3, 1: 5, 2: 7, 3: 7, 4: 9}[s]
        advance(need)
        for way, length in zip((1, -1), lengths(q)):
            ring, send, recv, device = (
                (plus, zp_send, zp_recv, z_above) if way == 1 else (minus, zm_send, zm_recv, z_below)
            )
            if s >= length:
                continue
            value = partial(q, (way * (length - s)) % NZ)
            if s == 0:
                first[q, (1 - way) // 2] = value
                source = first.at[q, (1 - way) // 2]
            else:
                arrived(ring.at[q, s - 1], recv.at[q, s - 1])
                ring[q, s - 1] = ring[q, s - 1] + value
                source = ring.at[q, s - 1]
            remote(source, ring.at[q, s], send.at[q, s], recv.at[q, s], device)

    def finish(q):
        advance(9)
        value = partial(q, 0)
        up, down = lengths(q)
        arrived(plus.at[q, up - 1], zp_recv.at[q, up - 1])
        arrived(minus.at[q, down - 1], zm_recv.at[q, down - 1])
        final[q] = value + plus[q, up - 1] + minus[q, down - 1]
        half, part = q // 2, q % 2
        stays = (c // 2 == r) & (c % 2 == half)
        target = mirrored.at[c % 2, part]

        @pl.when(stays)
        def _():
            pltpu.make_async_copy(final.at[q], target, m_recv.at[c % 2, part]).start()

        @pl.when(jnp.logical_not(stays))
        def _():
            pltpu.make_async_remote_copy(
                src_ref=final.at[q], dst_ref=target, send_sem=m_send.at[q], recv_sem=m_recv.at[c % 2, part],
                device_id=(c // 2, 2 * r + half), device_id_type=MESH,
            ).start()

    for slot in range(STAGGER * (CH - 1) + 5):
        for q in range(CH):
            s = slot - STAGGER * q
            if 0 <= s < 4:
                step_of(q, s)
            elif s == 4:
                finish(q)

    for half in range(2):
        for part in range(2):
            arrived(mirrored.at[half, part], m_recv.at[half, part])
            turned = mirrored[half, part].T
            for piece in range(2):
                q = 2 * half + piece
                out_ref[rows(q), part * BS:(part + 1) * BS] = (
                    final[q, :, part * BS:(part + 1) * BS] + turned[piece * QR:(piece + 1) * QR]
                )
    for copy in sends:
        copy.wait_send()
    for q in range(CH):
        @pl.when(jnp.logical_not((c // 2 == r) & (c % 2 == q // 2)))
        def _():
            arrived(final.at[q], m_send.at[q])


def offsets_of(block_columns):
    per_device = block_columns.shape[0]
    blocks = per_device * lax.axis_size("col")
    first = lax.axis_index("col") * per_device
    own = first + jnp.arange(per_device, dtype=jnp.int32)[:, None, None]
    offset = (block_columns[:, None, :] - own + blocks // 2) % blocks - blocks // 2
    asked = jnp.arange(OFFS, dtype=jnp.int32)[None, :, None] - 17
    hit = offset == asked
    where = jnp.sum(jnp.where(hit, jnp.arange(K, dtype=jnp.int32)[None, None, :], 0), axis=2)
    return where, jnp.any(hit, axis=2).astype(jnp.float32)


def local(ci_coeffs, h_blocks, block_columns):
    where, flag = offsets_of(block_columns)
    f32, bf16 = jnp.float32, jnp.bfloat16
    dma = pltpu.SemaphoreType.DMA
    return pl.pallas_call(
        kernel,
        out_shape=jax.ShapeDtypeStruct((ROWS, COLS), f32),
        in_specs=[
            pl.BlockSpec(memory_space=pltpu.SMEM),
            pl.BlockSpec(memory_space=pltpu.SMEM),
            pl.BlockSpec(memory_space=pl.ANY),
            pl.BlockSpec(memory_space=pl.ANY),
        ],
        out_specs=pl.BlockSpec(memory_space=pltpu.VMEM),
        scratch_shapes=[
            pltpu.VMEM((3, ROWS, COLS), f32),
            pltpu.VMEM((2, K, BS, BS), f32),
            pltpu.VMEM((17, 4, 2, 32, COLS), f32),
            pltpu.VMEM((9, 4, 2, 32, COLS), f32),
            pltpu.VMEM((8, 2, COLS, COLS), bf16),
            pltpu.VMEM((9, 2, COLS, COLS), bf16),
            pltpu.VMEM((3, 2, ROWS, COLS), bf16),
            pltpu.VMEM((CH, 2, QR, COLS), f32),
            pltpu.VMEM((CH, 4, QR, COLS), f32),
            pltpu.VMEM((CH, 4, QR, COLS), f32),
            pltpu.VMEM((CH, QR, COLS), f32),
            pltpu.VMEM((2, 2, QR, COLS), f32),
            dma((2,)),
            dma((2, CH)), dma((2, CH)),
            dma((9,)), dma((9,)),
            dma((9, 3)), dma((9, 3)),
            dma((9,)), dma((9,)),
            dma((CH, 4)), dma((CH, 4)),
            dma((CH, 4)), dma((CH, 4)),
            dma((CH,)), dma((2, 2)),
        ],
        compiler_params=pltpu.CompilerParams(
            collective_id=0, has_side_effects=True, vmem_limit_bytes=48 * 2**20
        ),
        cost_estimate=pl.CostEstimate(flops=7 * 10**9, bytes_accessed=5 * 2**20, transcendentals=0),
    )(where, flag, ci_coeffs, h_blocks)


def solution(mesh):
    return jax.shard_map(
        local,
        mesh=mesh,
        in_specs=(P("row", "col"), P("col", None, None, None), P("col", None)),
        out_specs=P("row", "col"),
        check_vma=False,
    )
```

```python
import jax
import jax.numpy as jnp
from jax import lax
from jax.experimental import pallas as pl
from jax.experimental.pallas import tpu as pltpu
from jax.sharding import PartitionSpec as P

NX, NYL, NZ = 4, 4, 8
BS = 128
K = 24
STAGGER = 1
CH = 4
ROWS = 512
COLS = 256
QR = ROWS // CH
OFFS = 36
MESH = pl.DeviceIdType.MESH
ORDER = (4, 3, 5, 2, 6, 1, 7, 0, 8)
PLACE = {d: p for p, d in enumerate(ORDER)}
BATCHES = ((0, 3), (3, 5), (5, 9))


def split(value):
    high = value.astype(jnp.bfloat16)
    low = (value - high.astype(jnp.float32)).astype(jnp.bfloat16)
    return high, low


def dot(a, b):
    return jnp.dot(a, b, preferred_element_type=jnp.float32)


def kernel(
    where_ref, flag_ref, c_hbm, h_hbm, out_ref,
    cbuf, hraw, placed, hy, wown, wnear, xb, first, plus, minus, final, via, mirrored,
    loc_sem, yc_send, yc_recv, yh_send, yh_recv, xh_send, xh_recv, kh_send, kh_recv,
    zp_send, zp_recv, zm_send, zm_recv, m_send, m_recv, v_send, v_recv,
):
    r = lax.axis_index("row")
    c = lax.axis_index("col")
    y_hi, x, core = r // 8, (r // 2) % NX, r % 2
    y_lo, z = c // NZ, c % NZ
    y = y_hi * NYL + y_lo

    def physical(step):
        other = (y + step + 2 * NYL) % (2 * NYL)
        return (other // NYL) * 8 + x * 2 + core, (other % NYL) * NZ + z

    def along_x(step):
        return y_hi * 8 + ((x + step) % NX) * 2 + core, c

    col_above = (r, ((y_lo + 1) % NYL) * NZ + z)
    col_below = (r, ((y_lo + NYL - 1) % NYL) * NZ + z)
    y_above, y_below = physical(1), physical(-1)
    z_above = (r, y_lo * NZ + (z + 1) % NZ)
    z_below = (r, y_lo * NZ + (z + NZ - 1) % NZ)
    sibling = (y_hi * 8 + x * 2 + 1 - core, c)
    peers = [along_x(step) for step in (1, 2, 3)]

    def beside(row):
        return row + 6 - 4 * ((row // 2) % NX)

    neighbour = (beside(r), c)
    straight = [(c // 2, 2 * r + half) for half in range(2)]
    onward = [(c // 2, 2 * beside(r) + half) for half in range(2)]
    sources = straight + [(beside(c // 2), 2 * r + half) for half in range(2)]

    def elsewhere(device):
        return (device[0] != r) | (device[1] != c)

    get_c = pltpu.make_async_copy(c_hbm, cbuf.at[0], loc_sem.at[0])
    get_h = pltpu.make_async_copy(h_hbm, hraw, loc_sem.at[1])
    get_c.start()
    get_h.start()

    barrier = pltpu.get_barrier_semaphore()
    fixed = [col_above, col_below, y_above, y_below, z_above, z_below, sibling] + peers
    for device in fixed:
        pl.semaphore_signal(barrier, inc=1, device_id=device, device_id_type=MESH)
    for device in sources:
        @pl.when(elsewhere(device))
        def _():
            pl.semaphore_signal(barrier, inc=1, device_id=device, device_id_type=MESH)
    replies = len(fixed)
    for device in straight + onward:
        replies = replies + elsewhere(device).astype(jnp.int32)
    get_c.wait()
    get_h.wait()
    pl.semaphore_wait(barrier, replies)

    sends = []

    def remote(src, dst, send_sem, recv_sem, device):
        copy = pltpu.make_async_remote_copy(
            src_ref=src, dst_ref=dst, send_sem=send_sem, recv_sem=recv_sem,
            device_id=device, device_id_type=MESH,
        )
        copy.start()
        sends.append(copy)

    routed = []

    def route(src, dst, send_sem, recv_sem, device):
        @pl.when(jnp.logical_not(elsewhere(device)))
        def _():
            pltpu.make_async_copy(src, dst, recv_sem).start()

        @pl.when(elsewhere(device))
        def _():
            pltpu.make_async_remote_copy(
                src_ref=src, dst_ref=dst, send_sem=send_sem, recv_sem=recv_sem,
                device_id=device, device_id_type=MESH,
            ).start()

        routed.append((src, send_sem, elsewhere(device)))

    def arrived(ref, sem):
        pltpu.make_async_copy(ref, ref, sem).wait()

    def rows(q):
        return pl.ds(q * QR, QR)

    def send_c(q):
        remote(cbuf.at[0, rows(q)], cbuf.at[2, rows(q)], yc_send.at[0, q], yc_recv.at[1, q], col_above)
        remote(cbuf.at[0, rows(q)], cbuf.at[1, rows(q)], yc_send.at[1, q], yc_recv.at[0, q], col_below)

    def place(index):
        for j in range(2):
            for e in range(2):
                at = 2 * (index - 8) + e - j + 17
                block = hraw[j, where_ref[j, at]] * flag_ref[j, at]
                placed[index, 2 * j:2 * j + 2, :, :, e * BS:(e + 1) * BS] = block.reshape(2, 2, 32, BS)

    def inside(d):
        return z + d < NZ

    def send_h(slot):
        if slot == 0:
            index, device = 0, y_below
        elif slot == 8:
            index, device = 16, y_above
        else:
            index = jnp.where(inside(slot), slot, slot + 8)
            device = tuple(jnp.where(inside(slot), b, a) for a, b in zip(y_above, y_below))
        p = PLACE[slot]
        remote(placed.at[index, x, core], hy.at[p, x, core], yh_send.at[p], yh_recv.at[p], device)

    send_c(0)
    for slot in ORDER:
        if slot == 8:
            place(16)
        else:
            place(slot)
            place(slot + 8)
        send_h(slot)
    def batch(b):
        return pl.ds(BATCHES[b][0], BATCHES[b][1] - BATCHES[b][0])

    def spread_x(b):
        for p in range(*BATCHES[b]):
            arrived(hy.at[p, x, core], yh_recv.at[p])
        for step in range(3):
            piece = hy.at[batch(b), x, core]
            remote(piece, piece, xh_send.at[b, step], xh_recv.at[b, step], peers[step])

    def spread_core(b):
        for step in range(3):
            arrived(hy.at[batch(b), 0, 0], xh_recv.at[b, step])
        piece = hy.at[batch(b), :, core]
        remote(piece, piece, kh_send.at[b], kh_recv.at[b], sibling)

    def split_own(d):
        index = 8 if d == 0 else jnp.where(inside(d), d + 8, d)
        high, low = split(placed[index].reshape(COLS, COLS))
        wown[d, 0] = high
        wown[d, 1] = low

    def split_near(b):
        arrived(hy.at[batch(b), :, 0], kh_recv.at[b])
        for p in range(*BATCHES[b]):
            high, low = split(hy[p].reshape(COLS, COLS))
            wnear[p, 0] = high
            wnear[p, 1] = low

    def split_c(which, q):
        high, low = split(cbuf[which, rows(q)])
        xb[which, 0, rows(q)] = high
        xb[which, 1, rows(q)] = low

    for slot in ORDER:
        if slot < 8:
            split_own(slot)
    for q in range(CH):
        split_c(0, q)

    tasks = [
        [(spread_x, 0), (send_c, 1), (spread_x, 1), (spread_core, 0), (spread_x, 2), (spread_core, 1), (split_near, 0)],
        [(split_near, 1), (spread_core, 2)],
        [(split_near, 2)],
    ]

    def advance(upto):
        while len(tasks) > 3 - upto:
            for stage, b in tasks.pop(0):
                stage(b)

    def product(which, weights, q):
        high, low = xb[which, 0, rows(q)], xb[which, 1, rows(q)]
        return dot(high, weights[0]) + dot(high, weights[1]) + dot(low, weights[0])

    def partial(q, d):
        total = product(0, wown.at[d], q)
        if d == 0:
            return total + product(1, wnear.at[PLACE[0]], q) + product(2, wnear.at[PLACE[8]], q)
        return total + product(jnp.where(inside(d), 1, 2), wnear.at[PLACE[d]], q)

    def lengths(q):
        return (4, 3) if q % 2 == 0 else (3, 4)

    def step_of(q, s):
        advance(min(s + 1, 3))
        if s == 0:
            for which in (1, 2):
                arrived(cbuf.at[which, rows(q)], yc_recv.at[which - 1, q])
                split_c(which, q)
            if q + 2 < CH:
                send_c(q + 2)
        for way, length in zip((1, -1), lengths(q)):
            ring, send, recv, device = (
                (plus, zp_send, zp_recv, z_above) if way == 1 else (minus, zm_send, zm_recv, z_below)
            )
            if s >= length:
                continue
            value = partial(q, (way * (length - s)) % NZ)
            if s == 0:
                first[q, (1 - way) // 2] = value
                source = first.at[q, (1 - way) // 2]
            else:
                arrived(ring.at[q, s - 1], recv.at[q, s - 1])
                ring[q, s - 1] = ring[q, s - 1] + value
                source = ring.at[q, s - 1]
            remote(source, ring.at[q, s], send.at[q, s], recv.at[q, s], device)

    def finish(q):
        advance(3)
        value = partial(q, 0)
        up, down = lengths(q)
        arrived(plus.at[q, up - 1], zp_recv.at[q, up - 1])
        arrived(minus.at[q, down - 1], zm_recv.at[q, down - 1])
        final[rows(q)] = value + plus[q, up - 1] + minus[q, down - 1]

    def part_rows(part):
        return pl.ds(part * BS, BS)

    def mirror_out(m):
        half, part = m // 2, m % 2
        src = final.at[part_rows(m)]
        if part == 0:
            remote(src, via.at[half], m_send.at[m], v_recv.at[half], neighbour)
        else:
            route(src, mirrored.at[c % 2, part_rows(part)], m_send.at[m], m_recv.at[c % 2, part], straight[half])

    def mirror_on(m):
        half, part = m // 2, m % 2
        if part == 0:
            arrived(via.at[half], v_recv.at[half])
            route(via.at[half], mirrored.at[c % 2, part_rows(part)], v_send.at[half], m_recv.at[c % 2, part], onward[half])

    group = CH // 4
    for slot in range(STAGGER * (CH - 1) + 6):
        for q in range(CH):
            s = slot - STAGGER * q
            if 0 <= s < 4:
                step_of(q, s)
            elif s == 4:
                finish(q)
                if q % group == group - 1:
                    mirror_out(q // group)
            elif s == 5 and q % group == group - 1:
                mirror_on(q // group)

    for half in range(2):
        for part in range(2):
            arrived(mirrored.at[half, part_rows(part)], m_recv.at[half, part])
            turned = mirrored[half, part_rows(part)].T
            at = pl.ds(half * COLS, COLS)
            out_ref[at, part * BS:(part + 1) * BS] = final[at, part * BS:(part + 1) * BS] + turned
    for copy in sends:
        copy.wait_send()
    for src, send_sem, role in routed:
        @pl.when(role)
        def _():
            arrived(src, send_sem)


def offsets_of(block_columns):
    per_device = block_columns.shape[0]
    blocks = per_device * lax.axis_size("col")
    first = lax.axis_index("col") * per_device
    own = first + jnp.arange(per_device, dtype=jnp.int32)[:, None, None]
    offset = (block_columns[:, None, :] - own + blocks // 2) % blocks - blocks // 2
    asked = jnp.arange(OFFS, dtype=jnp.int32)[None, :, None] - 17
    hit = offset == asked
    where = jnp.sum(jnp.where(hit, jnp.arange(K, dtype=jnp.int32)[None, None, :], 0), axis=2)
    return where, jnp.any(hit, axis=2).astype(jnp.float32)


def local(ci_coeffs, h_blocks, block_columns):
    where, flag = offsets_of(block_columns)
    f32, bf16 = jnp.float32, jnp.bfloat16
    dma = pltpu.SemaphoreType.DMA
    return pl.pallas_call(
        kernel,
        out_shape=jax.ShapeDtypeStruct((ROWS, COLS), f32),
        in_specs=[
            pl.BlockSpec(memory_space=pltpu.SMEM),
            pl.BlockSpec(memory_space=pltpu.SMEM),
            pl.BlockSpec(memory_space=pltpu.HBM),
            pl.BlockSpec(memory_space=pltpu.HBM),
        ],
        out_specs=pl.BlockSpec(memory_space=pltpu.VMEM),
        scratch_shapes=[
            pltpu.VMEM((3, ROWS, COLS), f32),
            pltpu.VMEM((2, K, BS, BS), f32),
            pltpu.VMEM((17, 4, 2, 32, COLS), f32),
            pltpu.VMEM((9, 4, 2, 32, COLS), f32),
            pltpu.VMEM((8, 2, COLS, COLS), bf16),
            pltpu.VMEM((9, 2, COLS, COLS), bf16),
            pltpu.VMEM((3, 2, ROWS, COLS), bf16),
            pltpu.VMEM((CH, 2, QR, COLS), f32),
            pltpu.VMEM((CH, 4, QR, COLS), f32),
            pltpu.VMEM((CH, 4, QR, COLS), f32),
            pltpu.VMEM((ROWS, COLS), f32),
            pltpu.VMEM((2, BS, COLS), f32),
            pltpu.VMEM((2, 2 * BS, COLS), f32),
            dma((2,)),
            dma((2, CH)), dma((2, CH)),
            dma((9,)), dma((9,)),
            dma((3, 3)), dma((3, 3)),
            dma((3,)), dma((3,)),
            dma((CH, 4)), dma((CH, 4)),
            dma((CH, 4)), dma((CH, 4)),
            dma((4,)), dma((2, 2)),
            dma((2,)), dma((2,)),
        ],
        compiler_params=pltpu.CompilerParams(
            collective_id=0, has_side_effects=True, vmem_limit_bytes=60 * 2**20
        ),
        cost_estimate=pl.CostEstimate(flops=7 * 10**9, bytes_accessed=5 * 2**20, transcendentals=0),
    )(where, flag, ci_coeffs, h_blocks)


def solution(mesh):
    return jax.shard_map(
        local,
        mesh=mesh,
        in_specs=(P("row", "col"), P("col", None, None, None), P("col", None)),
        out_specs=P("row", "col"),
        check_vma=False,
    )
```

```python
import jax
import jax.numpy as jnp
from jax import lax
from jax.experimental import pallas as pl
from jax.experimental.pallas import tpu as pltpu
from jax.sharding import PartitionSpec as P

NX, NYL, NZ = 4, 4, 8
BS = 128
K = 24
STAGGER = 1
CH = 4
ROWS = 512
COLS = 256
QR = ROWS // CH
SUB = 2
SR = QR // SUB
OFFS = 36
MESH = pl.DeviceIdType.MESH
ORDER = (4, 3, 5, 2, 6, 1, 7, 0, 8)
PLACE = {d: p for p, d in enumerate(ORDER)}
BATCHES = ((0, 3), (3, 5), (5, 9))


def split(value):
    high = value.astype(jnp.bfloat16)
    low = (value - high.astype(jnp.float32)).astype(jnp.bfloat16)
    return high, low


def dot(a, b):
    return jnp.dot(a, b, preferred_element_type=jnp.float32)


def kernel(
    where_ref, flag_ref, c_hbm, h_hbm, out_ref,
    cbuf, hraw, placed, hy, wown, wnear, xb, sums, plus, minus, final, via, mirrored,
    loc_sem, yc_send, yc_recv, yh_send, yh_recv, xh_send, xh_recv, kh_send, kh_recv,
    zp_send, zp_recv, zm_send, zm_recv, m_send, m_recv, v_send, v_recv,
):
    r = lax.axis_index("row")
    c = lax.axis_index("col")
    y_hi, x, core = r // 8, (r // 2) % NX, r % 2
    y_lo, z = c // NZ, c % NZ
    y = y_hi * NYL + y_lo

    def physical(step):
        other = (y + step + 2 * NYL) % (2 * NYL)
        return (other // NYL) * 8 + x * 2 + core, (other % NYL) * NZ + z

    def along_x(step):
        return y_hi * 8 + ((x + step) % NX) * 2 + core, c

    col_above = (r, ((y_lo + 1) % NYL) * NZ + z)
    col_below = (r, ((y_lo + NYL - 1) % NYL) * NZ + z)
    y_above, y_below = physical(1), physical(-1)
    z_above = (r, y_lo * NZ + (z + 1) % NZ)
    z_below = (r, y_lo * NZ + (z + NZ - 1) % NZ)
    sibling = (y_hi * 8 + x * 2 + 1 - core, c)
    peers = [along_x(step) for step in (1, 2, 3)]

    def beside(row):
        return row + 6 - 4 * ((row // 2) % NX)

    neighbour = (beside(r), c)
    straight = [(c // 2, 2 * r + half) for half in range(2)]
    onward = [(c // 2, 2 * beside(r) + half) for half in range(2)]
    sources = straight + [(beside(c // 2), 2 * r + half) for half in range(2)]

    def elsewhere(device):
        return (device[0] != r) | (device[1] != c)

    get_c = pltpu.make_async_copy(c_hbm, cbuf.at[0], loc_sem.at[0])
    get_h = pltpu.make_async_copy(h_hbm, hraw, loc_sem.at[1])
    get_c.start()
    get_h.start()

    barrier = pltpu.get_barrier_semaphore()
    fixed = [col_above, col_below, y_above, y_below, z_above, z_below, sibling] + peers
    for device in fixed:
        pl.semaphore_signal(barrier, inc=1, device_id=device, device_id_type=MESH)
    for device in sources:
        @pl.when(elsewhere(device))
        def _():
            pl.semaphore_signal(barrier, inc=1, device_id=device, device_id_type=MESH)
    replies = len(fixed)
    for device in straight + onward:
        replies = replies + elsewhere(device).astype(jnp.int32)
    get_c.wait()
    get_h.wait()
    pl.semaphore_wait(barrier, replies)

    sends = []

    def remote(src, dst, send_sem, recv_sem, device):
        copy = pltpu.make_async_remote_copy(
            src_ref=src, dst_ref=dst, send_sem=send_sem, recv_sem=recv_sem,
            device_id=device, device_id_type=MESH,
        )
        copy.start()
        sends.append(copy)

    routed = []

    def route(src, dst, send_sem, recv_sem, device):
        @pl.when(jnp.logical_not(elsewhere(device)))
        def _():
            pltpu.make_async_copy(src, dst, recv_sem).start()

        @pl.when(elsewhere(device))
        def _():
            pltpu.make_async_remote_copy(
                src_ref=src, dst_ref=dst, send_sem=send_sem, recv_sem=recv_sem,
                device_id=device, device_id_type=MESH,
            ).start()

        routed.append((src, send_sem, elsewhere(device)))

    def arrived(ref, sem):
        pltpu.make_async_copy(ref, ref, sem).wait()

    def rows(q):
        return pl.ds(q * QR, QR)

    def send_c(q):
        remote(cbuf.at[0, rows(q)], cbuf.at[2, rows(q)], yc_send.at[0, q], yc_recv.at[1, q], col_above)
        remote(cbuf.at[0, rows(q)], cbuf.at[1, rows(q)], yc_send.at[1, q], yc_recv.at[0, q], col_below)

    def place(index):
        for j in range(2):
            for e in range(2):
                at = 2 * (index - 8) + e - j + 17
                block = hraw[j, where_ref[j, at]] * flag_ref[j, at]
                placed[index, 2 * j:2 * j + 2, :, :, e * BS:(e + 1) * BS] = block.reshape(2, 2, 32, BS)

    def inside(d):
        return z + d < NZ

    def send_h(slot):
        if slot == 0:
            index, device = 0, y_below
        elif slot == 8:
            index, device = 16, y_above
        else:
            index = jnp.where(inside(slot), slot, slot + 8)
            device = tuple(jnp.where(inside(slot), b, a) for a, b in zip(y_above, y_below))
        p = PLACE[slot]
        remote(placed.at[index, x, core], hy.at[p, x, core], yh_send.at[p], yh_recv.at[p], device)

    for slot in ORDER:
        if slot == 8:
            place(16)
        else:
            place(slot)
            place(slot + 8)
        send_h(slot)
        if slot == ORDER[2]:
            send_c(0)
    def batch(b):
        return pl.ds(BATCHES[b][0], BATCHES[b][1] - BATCHES[b][0])

    def spread_x(b):
        for p in range(*BATCHES[b]):
            arrived(hy.at[p, x, core], yh_recv.at[p])
        for step in range(3):
            piece = hy.at[batch(b), x, core]
            remote(piece, piece, xh_send.at[b, step], xh_recv.at[b, step], peers[step])

    def spread_core(b):
        for step in range(3):
            arrived(hy.at[batch(b), 0, 0], xh_recv.at[b, step])
        piece = hy.at[batch(b), :, core]
        remote(piece, piece, kh_send.at[b], kh_recv.at[b], sibling)

    def split_own(d):
        index = 8 if d == 0 else jnp.where(inside(d), d + 8, d)
        high, low = split(placed[index].reshape(COLS, COLS))
        wown[d, 0] = high
        wown[d, 1] = low

    def split_near(b):
        arrived(hy.at[batch(b), :, 0], kh_recv.at[b])
        for p in range(*BATCHES[b]):
            high, low = split(hy[p].reshape(COLS, COLS))
            wnear[p, 0] = high
            wnear[p, 1] = low

    def split_c(which, q):
        high, low = split(cbuf[which, rows(q)])
        xb[which, 0, rows(q)] = high
        xb[which, 1, rows(q)] = low

    for slot in ORDER:
        if slot < 8:
            split_own(slot)
    for q in range(CH):
        split_c(0, q)

    tasks = [
        [(spread_x, 0), (send_c, 1), (spread_x, 1), (spread_core, 0), (spread_x, 2), (spread_core, 1), (split_near, 0)],
        [(split_near, 1), (spread_core, 2)],
        [(split_near, 2)],
    ]

    def advance(upto):
        while len(tasks) > 3 - upto:
            for stage, b in tasks.pop(0):
                stage(b)

    def product(which, weights, q):
        high, low = xb[which, 0, rows(q)], xb[which, 1, rows(q)]
        return dot(high, weights[0]) + dot(high, weights[1]) + dot(low, weights[0])

    def partial(q, d):
        total = product(0, wown.at[d], q)
        if d == 0:
            return total + product(1, wnear.at[PLACE[0]], q) + product(2, wnear.at[PLACE[8]], q)
        return total + product(jnp.where(inside(d), 1, 2), wnear.at[PLACE[d]], q)

    def compute(g, targets):
        for d in targets:
            sums[d, rows(g)] = partial(g, d)

    def lengths(q):
        return (4, 3) if q % 2 == 0 else (3, 4)

    def piece_rows(q):
        return pl.ds(q * SR, SR)

    def step_of(g, s):
        if s == 0:
            advance(1)
            for which in (1, 2):
                arrived(cbuf.at[which, rows(g)], yc_recv.at[which - 1, g])
                split_c(which, g)
            if g + 2 < CH:
                send_c(g + 2)
            compute(g, (4, 5, 3))
        for q in range(SUB * g, SUB * g + SUB):
            for way, length in zip((1, -1), lengths(q)):
                ring, send, recv, device = (
                    (plus, zp_send, zp_recv, z_above) if way == 1 else (minus, zm_send, zm_recv, z_below)
                )
                if s >= length:
                    continue
                d = (way * (length - s)) % NZ
                if s == 0:
                    source = sums.at[d, piece_rows(q)]
                else:
                    arrived(ring.at[q, s - 1], recv.at[q, s - 1])
                    ring[q, s - 1] = ring[q, s - 1] + sums[d, piece_rows(q)]
                    source = ring.at[q, s - 1]
                remote(source, ring.at[q, s], send.at[q, s], recv.at[q, s], device)
        if s == 0:
            advance(2)
            compute(g, (2, 6))
        if s == 1:
            advance(3)
            compute(g, (1, 7, 0))

    def finish(g):
        for q in range(SUB * g, SUB * g + SUB):
            up, down = lengths(q)
            arrived(plus.at[q, up - 1], zp_recv.at[q, up - 1])
            arrived(minus.at[q, down - 1], zm_recv.at[q, down - 1])
            final[piece_rows(q)] = sums[0, piece_rows(q)] + plus[q, up - 1] + minus[q, down - 1]

    def part_rows(part):
        return pl.ds(part * BS, BS)

    def split_rows(part, way):
        return pl.ds(part * BS + way * (BS // 2), BS // 2)

    def mirror_out(m):
        half, part = m // 2, m % 2
        remote(final.at[split_rows(m, 0)], via.at[m], m_send.at[m, 0], v_recv.at[m], neighbour)
        route(final.at[split_rows(m, 1)], mirrored.at[c % 2, split_rows(part, 1)], m_send.at[m, 1],
              m_recv.at[c % 2, part, 1], straight[half])

    def mirror_on(m):
        half, part = m // 2, m % 2
        arrived(via.at[m], v_recv.at[m])
        route(via.at[m], mirrored.at[c % 2, split_rows(part, 0)], v_send.at[m], m_recv.at[c % 2, part, 0], onward[half])

    group = CH // 4
    for slot in range(STAGGER * (CH - 1) + 6):
        for q in range(CH):
            s = slot - STAGGER * q
            if 0 <= s < 4:
                step_of(q, s)
            elif s == 4:
                finish(q)
                if q % group == group - 1:
                    mirror_out(q // group)
            elif s == 5 and q % group == group - 1:
                mirror_on(q // group)

    for half in range(2):
        for part in range(2):
            for way in range(2):
                arrived(mirrored.at[half, split_rows(part, way)], m_recv.at[half, part, way])
            turned = mirrored[half, part_rows(part)].T
            at = pl.ds(half * COLS, COLS)
            out_ref[at, part * BS:(part + 1) * BS] = final[at, part * BS:(part + 1) * BS] + turned
    for copy in sends:
        copy.wait_send()
    for src, send_sem, role in routed:
        @pl.when(role)
        def _():
            arrived(src, send_sem)


def offsets_of(block_columns):
    per_device = block_columns.shape[0]
    blocks = per_device * lax.axis_size("col")
    first = lax.axis_index("col") * per_device
    own = first + jnp.arange(per_device, dtype=jnp.int32)[:, None, None]
    offset = ((block_columns[:, None, :] - own + blocks // 2) & (blocks - 1)) - blocks // 2
    asked = jnp.arange(OFFS, dtype=jnp.int32)[None, :, None] - 17
    hit = offset == asked
    where = jnp.sum(jnp.where(hit, jnp.arange(K, dtype=jnp.int32)[None, None, :], 0), axis=2)
    return where, jnp.any(hit, axis=2).astype(jnp.float32)


def local(ci_coeffs, h_blocks, block_columns):
    where, flag = offsets_of(block_columns)
    f32, bf16 = jnp.float32, jnp.bfloat16
    dma = pltpu.SemaphoreType.DMA
    return pl.pallas_call(
        kernel,
        out_shape=jax.ShapeDtypeStruct((ROWS, COLS), f32),
        in_specs=[
            pl.BlockSpec(memory_space=pltpu.SMEM),
            pl.BlockSpec(memory_space=pltpu.SMEM),
            pl.BlockSpec(memory_space=pltpu.HBM),
            pl.BlockSpec(memory_space=pltpu.HBM),
        ],
        out_specs=pl.BlockSpec(memory_space=pltpu.VMEM),
        scratch_shapes=[
            pltpu.VMEM((3, ROWS, COLS), f32),
            pltpu.VMEM((2, K, BS, BS), f32),
            pltpu.VMEM((17, 4, 2, 32, COLS), f32),
            pltpu.VMEM((9, 4, 2, 32, COLS), f32),
            pltpu.VMEM((8, 2, COLS, COLS), bf16),
            pltpu.VMEM((9, 2, COLS, COLS), bf16),
            pltpu.VMEM((3, 2, ROWS, COLS), bf16),
            pltpu.VMEM((NZ, ROWS, COLS), f32),
            pltpu.VMEM((CH * SUB, 4, SR, COLS), f32),
            pltpu.VMEM((CH * SUB, 4, SR, COLS), f32),
            pltpu.VMEM((ROWS, COLS), f32),
            pltpu.VMEM((4, BS // 2, COLS), f32),
            pltpu.VMEM((2, 2 * BS, COLS), f32),
            dma((2,)),
            dma((2, CH)), dma((2, CH)),
            dma((9,)), dma((9,)),
            dma((3, 3)), dma((3, 3)),
            dma((3,)), dma((3,)),
            dma((CH * SUB, 4)), dma((CH * SUB, 4)),
            dma((CH * SUB, 4)), dma((CH * SUB, 4)),
            dma((4, 2)), dma((2, 2, 2)),
            dma((4,)), dma((4,)),
        ],
        compiler_params=pltpu.CompilerParams(
            collective_id=0, has_side_effects=True, vmem_limit_bytes=60 * 2**20
        ),
        cost_estimate=pl.CostEstimate(flops=7 * 10**9, bytes_accessed=5 * 2**20, transcendentals=0),
    )(where, flag, ci_coeffs, h_blocks)


def solution(mesh):
    return jax.shard_map(
        local,
        mesh=mesh,
        in_specs=(P("row", "col"), P("col", None, None, None), P("col", None)),
        out_specs=P("row", "col"),
        check_vma=False,
    )
```

```python
import jax
import jax.numpy as jnp
from jax import lax
from jax.experimental import pallas as pl
from jax.experimental.pallas import tpu as pltpu
from jax.sharding import PartitionSpec as P

NX, NYL, NZ = 4, 4, 8
BS = 128
K = 24
STAGGER = 1
CH = 4
ROWS = 512
COLS = 256
QR = ROWS // CH
SUB = 2
SR = QR // SUB
OFFS = 36
MESH = pl.DeviceIdType.MESH
ORDER = (4, 3, 5, 2, 6, 1, 7, 0, 8)
PLACE = {d: p for p, d in enumerate(ORDER)}
BATCHES = ((0, 3), (3, 5), (5, 9))


def split(value):
    high = value.astype(jnp.bfloat16)
    low = (value - high.astype(jnp.float32)).astype(jnp.bfloat16)
    return high, low


def dot(a, b):
    return jnp.dot(a, b, preferred_element_type=jnp.float32)


def kernel(
    where_ref, flag_ref, c_hbm, h_hbm, out_ref,
    cbuf, hraw, placed, hy, wown, wnear, xb, sums, plus, minus, final, via, mirrored,
    loc_sem, yc_send, yc_recv, yh_send, yh_recv, xh_send, xh_recv, kh_send, kh_recv,
    zp_send, zp_recv, zm_send, zm_recv, m_send, m_recv, v_send, v_recv,
):
    r = lax.axis_index("row")
    c = lax.axis_index("col")
    y_hi, x, core = r // 8, (r // 2) % NX, r % 2
    y_lo, z = c // NZ, c % NZ
    y = y_hi * NYL + y_lo

    def physical(step):
        other = (y + step + 2 * NYL) % (2 * NYL)
        return (other // NYL) * 8 + x * 2 + core, (other % NYL) * NZ + z

    def along_x(step):
        return y_hi * 8 + ((x + step) % NX) * 2 + core, c

    col_above = (r, ((y_lo + 1) % NYL) * NZ + z)
    col_below = (r, ((y_lo + NYL - 1) % NYL) * NZ + z)
    y_above, y_below = physical(1), physical(-1)
    z_above = (r, y_lo * NZ + (z + 1) % NZ)
    z_below = (r, y_lo * NZ + (z + NZ - 1) % NZ)
    sibling = (y_hi * 8 + x * 2 + 1 - core, c)
    peers = [along_x(step) for step in (1, 2, 3)]

    def beside(row):
        return row + 6 - 4 * ((row // 2) % NX)

    neighbour = (beside(r), c)
    straight = [(c // 2, 2 * r + half) for half in range(2)]
    onward = [(c // 2, 2 * beside(r) + half) for half in range(2)]
    sources = straight + [(beside(c // 2), 2 * r + half) for half in range(2)]

    def elsewhere(device):
        return (device[0] != r) | (device[1] != c)

    get_c = pltpu.make_async_copy(c_hbm, cbuf.at[0], loc_sem.at[0])
    get_h = pltpu.make_async_copy(h_hbm, hraw, loc_sem.at[1])
    get_c.start()
    get_h.start()

    barrier = pltpu.get_barrier_semaphore()
    fixed = [col_above, col_below, y_above, y_below, z_above, z_below, sibling] + peers
    for device in fixed:
        pl.semaphore_signal(barrier, inc=1, device_id=device, device_id_type=MESH)
    for device in sources:
        @pl.when(elsewhere(device))
        def _():
            pl.semaphore_signal(barrier, inc=1, device_id=device, device_id_type=MESH)
    replies = len(fixed)
    for device in straight + onward:
        replies = replies + elsewhere(device).astype(jnp.int32)
    get_c.wait()
    get_h.wait()
    def place(index):
        for j in range(2):
            for e in range(2):
                at = 2 * (index - 8) + e - j + 17
                block = hraw[j, where_ref[j, at]] * flag_ref[j, at]
                placed[index, 2 * j:2 * j + 2, :, :, e * BS:(e + 1) * BS] = block.reshape(2, 2, 32, BS)

    for slot in ORDER[:3]:
        place(slot)
        place(slot + 8)
    pl.semaphore_wait(barrier, replies)

    sends = []

    def remote(src, dst, send_sem, recv_sem, device):
        copy = pltpu.make_async_remote_copy(
            src_ref=src, dst_ref=dst, send_sem=send_sem, recv_sem=recv_sem,
            device_id=device, device_id_type=MESH,
        )
        copy.start()
        sends.append(copy)

    routed = []

    def route(src, dst, send_sem, recv_sem, device):
        @pl.when(jnp.logical_not(elsewhere(device)))
        def _():
            pltpu.make_async_copy(src, dst, recv_sem).start()

        @pl.when(elsewhere(device))
        def _():
            pltpu.make_async_remote_copy(
                src_ref=src, dst_ref=dst, send_sem=send_sem, recv_sem=recv_sem,
                device_id=device, device_id_type=MESH,
            ).start()

        routed.append((src, send_sem, elsewhere(device)))

    def arrived(ref, sem):
        pltpu.make_async_copy(ref, ref, sem).wait()

    def rows(q):
        return pl.ds(q * QR, QR)

    def send_c(q):
        remote(cbuf.at[0, rows(q)], cbuf.at[2, rows(q)], yc_send.at[0, q], yc_recv.at[1, q], col_above)
        remote(cbuf.at[0, rows(q)], cbuf.at[1, rows(q)], yc_send.at[1, q], yc_recv.at[0, q], col_below)

    def inside(d):
        return z + d < NZ

    def send_h(slot):
        if slot == 0:
            index, device = 0, y_below
        elif slot == 8:
            index, device = 16, y_above
        else:
            index = jnp.where(inside(slot), slot, slot + 8)
            device = tuple(jnp.where(inside(slot), b, a) for a, b in zip(y_above, y_below))
        p = PLACE[slot]
        remote(placed.at[index, x, core], hy.at[p, x, core], yh_send.at[p], yh_recv.at[p], device)

    for slot in ORDER:
        if slot == 8:
            place(16)
        elif slot not in ORDER[:3]:
            place(slot)
            place(slot + 8)
        send_h(slot)
        if slot == ORDER[2]:
            send_c(0)
    def batch(b):
        return pl.ds(BATCHES[b][0], BATCHES[b][1] - BATCHES[b][0])

    def spread_x(b):
        for p in range(*BATCHES[b]):
            arrived(hy.at[p, x, core], yh_recv.at[p])
        for step in range(3):
            piece = hy.at[batch(b), x, core]
            remote(piece, piece, xh_send.at[b, step], xh_recv.at[b, step], peers[step])

    def spread_core(b):
        for step in range(3):
            arrived(hy.at[batch(b), 0, 0], xh_recv.at[b, step])
        piece = hy.at[batch(b), :, core]
        remote(piece, piece, kh_send.at[b], kh_recv.at[b], sibling)

    def split_own(d):
        index = 8 if d == 0 else jnp.where(inside(d), d + 8, d)
        high, low = split(placed[index].reshape(COLS, COLS))
        wown[d, 0] = high
        wown[d, 1] = low

    def split_near(b):
        arrived(hy.at[batch(b), :, 0], kh_recv.at[b])
        for p in range(*BATCHES[b]):
            high, low = split(hy[p].reshape(COLS, COLS))
            wnear[p, 0] = high
            wnear[p, 1] = low

    def split_c(which, q):
        high, low = split(cbuf[which, rows(q)])
        xb[which, 0, rows(q)] = high
        xb[which, 1, rows(q)] = low

    for slot in ORDER:
        if slot < 8:
            split_own(slot)
    for q in range(CH):
        split_c(0, q)

    tasks = [
        [(spread_x, 0), (send_c, 1), (spread_x, 1), (spread_core, 0), (spread_x, 2), (spread_core, 1), (split_near, 0)],
        [(split_near, 1), (spread_core, 2)],
        [(split_near, 2)],
    ]

    def advance(upto):
        while len(tasks) > 3 - upto:
            for stage, b in tasks.pop(0):
                stage(b)

    def product(which, weights, q):
        high, low = xb[which, 0, rows(q)], xb[which, 1, rows(q)]
        return dot(high, weights[0]) + dot(high, weights[1]) + dot(low, weights[0])

    def partial(q, d):
        total = product(0, wown.at[d], q)
        if d == 0:
            return total + product(1, wnear.at[PLACE[0]], q) + product(2, wnear.at[PLACE[8]], q)
        return total + product(jnp.where(inside(d), 1, 2), wnear.at[PLACE[d]], q)

    def compute(g, targets):
        for d in targets:
            sums[d, rows(g)] = partial(g, d)

    def lengths(q):
        return (4, 3) if q % 2 == 0 else (3, 4)

    def piece_rows(q):
        return pl.ds(q * SR, SR)

    def step_of(g, s):
        if s == 0:
            advance(1)
            for which in (1, 2):
                arrived(cbuf.at[which, rows(g)], yc_recv.at[which - 1, g])
                split_c(which, g)
            if g + 2 < CH:
                send_c(g + 2)
            compute(g, (4, 5, 3))
        for q in range(SUB * g, SUB * g + SUB):
            for way, length in zip((1, -1), lengths(q)):
                ring, send, recv, device = (
                    (plus, zp_send, zp_recv, z_above) if way == 1 else (minus, zm_send, zm_recv, z_below)
                )
                if s >= length:
                    continue
                d = (way * (length - s)) % NZ
                if s == 0:
                    source = sums.at[d, piece_rows(q)]
                else:
                    arrived(ring.at[q, s - 1], recv.at[q, s - 1])
                    ring[q, s - 1] = ring[q, s - 1] + sums[d, piece_rows(q)]
                    source = ring.at[q, s - 1]
                remote(source, ring.at[q, s], send.at[q, s], recv.at[q, s], device)
        if s == 0:
            advance(2)
            compute(g, (2, 6))
        if s == 1:
            advance(3)
            compute(g, (1, 7, 0))

    def finish(g):
        for q in range(SUB * g, SUB * g + SUB):
            up, down = lengths(q)
            arrived(plus.at[q, up - 1], zp_recv.at[q, up - 1])
            arrived(minus.at[q, down - 1], zm_recv.at[q, down - 1])
            final[piece_rows(q)] = sums[0, piece_rows(q)] + plus[q, up - 1] + minus[q, down - 1]

    def part_rows(part):
        return pl.ds(part * BS, BS)

    def split_rows(part, way):
        return pl.ds(part * BS + way * (BS // 2), BS // 2)

    def mirror_out(m):
        half, part = m // 2, m % 2
        remote(final.at[split_rows(m, 0)], via.at[m], m_send.at[m, 0], v_recv.at[m], neighbour)
        route(final.at[split_rows(m, 1)], mirrored.at[c % 2, split_rows(part, 1)], m_send.at[m, 1],
              m_recv.at[c % 2, part, 1], straight[half])

    def mirror_on(m):
        half, part = m // 2, m % 2
        arrived(via.at[m], v_recv.at[m])
        route(via.at[m], mirrored.at[c % 2, split_rows(part, 0)], v_send.at[m], m_recv.at[c % 2, part, 0], onward[half])

    group = CH // 4
    for slot in range(STAGGER * (CH - 1) + 6):
        for q in range(CH):
            s = slot - STAGGER * q
            if 0 <= s < 4:
                step_of(q, s)
            elif s == 4:
                finish(q)
                if q % group == group - 1:
                    mirror_out(q // group)
            elif s == 5 and q % group == group - 1:
                mirror_on(q // group)

    for half in range(2):
        for part in range(2):
            for way in range(2):
                arrived(mirrored.at[half, split_rows(part, way)], m_recv.at[half, part, way])
            turned = mirrored[half, part_rows(part)].T
            at = pl.ds(half * COLS, COLS)
            out_ref[at, part * BS:(part + 1) * BS] = final[at, part * BS:(part + 1) * BS] + turned
    for copy in sends:
        copy.wait_send()
    for src, send_sem, role in routed:
        @pl.when(role)
        def _():
            arrived(src, send_sem)


def offsets_of(block_columns):
    per_device = block_columns.shape[0]
    blocks = per_device * lax.axis_size("col")
    first = lax.axis_index("col") * per_device
    own = first + jnp.arange(per_device, dtype=jnp.int32)[:, None, None]
    offset = ((block_columns[:, None, :] - own + blocks // 2) & (blocks - 1)) - blocks // 2
    asked = jnp.arange(OFFS, dtype=jnp.int32)[None, :, None] - 17
    hit = offset == asked
    where = jnp.sum(jnp.where(hit, jnp.arange(K, dtype=jnp.int32)[None, None, :], 0), axis=2)
    return where, jnp.any(hit, axis=2).astype(jnp.float32)


def local(ci_coeffs, h_blocks, block_columns):
    where, flag = offsets_of(block_columns)
    f32, bf16 = jnp.float32, jnp.bfloat16
    dma = pltpu.SemaphoreType.DMA
    return pl.pallas_call(
        kernel,
        out_shape=jax.ShapeDtypeStruct((ROWS, COLS), f32),
        in_specs=[
            pl.BlockSpec(memory_space=pltpu.SMEM),
            pl.BlockSpec(memory_space=pltpu.SMEM),
            pl.BlockSpec(memory_space=pltpu.HBM),
            pl.BlockSpec(memory_space=pltpu.HBM),
        ],
        out_specs=pl.BlockSpec(memory_space=pltpu.VMEM),
        scratch_shapes=[
            pltpu.VMEM((3, ROWS, COLS), f32),
            pltpu.VMEM((2, K, BS, BS), f32),
            pltpu.VMEM((17, 4, 2, 32, COLS), f32),
            pltpu.VMEM((9, 4, 2, 32, COLS), f32),
            pltpu.VMEM((8, 2, COLS, COLS), bf16),
            pltpu.VMEM((9, 2, COLS, COLS), bf16),
            pltpu.VMEM((3, 2, ROWS, COLS), bf16),
            pltpu.VMEM((NZ, ROWS, COLS), f32),
            pltpu.VMEM((CH * SUB, 4, SR, COLS), f32),
            pltpu.VMEM((CH * SUB, 4, SR, COLS), f32),
            pltpu.VMEM((ROWS, COLS), f32),
            pltpu.VMEM((4, BS // 2, COLS), f32),
            pltpu.VMEM((2, 2 * BS, COLS), f32),
            dma((2,)),
            dma((2, CH)), dma((2, CH)),
            dma((9,)), dma((9,)),
            dma((3, 3)), dma((3, 3)),
            dma((3,)), dma((3,)),
            dma((CH * SUB, 4)), dma((CH * SUB, 4)),
            dma((CH * SUB, 4)), dma((CH * SUB, 4)),
            dma((4, 2)), dma((2, 2, 2)),
            dma((4,)), dma((4,)),
        ],
        compiler_params=pltpu.CompilerParams(
            collective_id=0, has_side_effects=True, vmem_limit_bytes=60 * 2**20
        ),
        cost_estimate=pl.CostEstimate(flops=7 * 10**9, bytes_accessed=5 * 2**20, transcendentals=0),
    )(where, flag, ci_coeffs, h_blocks)


def solution(mesh):
    return jax.shard_map(
        local,
        mesh=mesh,
        in_specs=(P("row", "col"), P("col", None, None, None), P("col", None)),
        out_specs=P("row", "col"),
        check_vma=False,
    )
```
